32 devices in a mesh: lat: 4 (over y, x), grp: 8 (over z, core).
Axes of the slice: x: 2, y: 2, z: 4, core: 2. Of those that a mesh axis runs over, the one named last changes fastest.
Arguments:
- fields: float32 [256, 30, 64, 128], P('grp', None, 'lat'), may hold values from -6 to 6
- diffusion: float32 [64, 128], P('lat'), may hold values from 0.12 to 0.245
- mixing: float32 [30, 30], replicated, may hold values from -0.08 to 1
- heating: float32 [30, 64, 128], P(None, 'lat'), may hold values from -2 to 2
- land_mask: int32 [64, 128], P('lat'), may hold values 0 or 1
- conv_weight: float32 [32, 27], replicated, may hold values from -1.25 to 1.25
- head_weight: float32 [32, 64, 128], P(None, 'lat'), may hold values from -0.01171875 to 0.01171875
- counts: int32 [256], replicated, may hold values from 0 to 32, as said below
- source: int32 [256], replicated, may hold values from 0 to 255, as said below
Outputs:
- new_fields: float32 [256, 30, 64, 128], P('grp', None, 'lat')
- scores: float32 [256], P('grp')
- slot_weight: float32 [256], P('grp')
The draws below stay inside these ranges and needn't reach their ends.
Inputs may be any that keep to these rules, and one draw needn't show every extreme that they name: Members 32 g to 32 g + 31 form group g. In every group exactly one member has a count of 2 or more and every group has a member of count 0; the counts sum to 256. source[s] = s where the member s has a count of 1 or more. Every slot s of count 0 takes the member of count 2 or more of one other group, the same group for all such slots of s's group, each group's such member is taken by the slots of exactly one other group, and a member of count c is taken by c - 1 slots.
All inputs are finite; a program needn't handle non-finite values. No bound on the sum of `land_mask` on one device may be relied on, other than what follows from the above.
Results may differ from the reference program's by a relative error of at most 0.0003.
Values sent between devices are 32-bit elements; how exact they have to be, the bound alone decides.
A program may use at most 128 MiB of HBM per device.

```python
import math
import jax
import jax.numpy as jnp
from jax import lax

NLON = 128
NLAT = 64
LEV = 10
FLD = 3
CH = 32
MEM_GRP = 32
STEPS = 4
MEMBERS = 256


def clone_plan(key):
    base_key = jax.random.fold_in(key, 911)
    key_hot, key_extra, key_order, key_force, key_rotate = jax.random.split(base_key, 5)
    groups = MEMBERS // MEM_GRP
    hot_slot = jax.random.randint(key_hot, (groups,), 0, MEM_GRP)
    extra = jax.random.randint(key_extra, (groups,), 1, MEM_GRP)
    forced = jax.random.randint(key_force, (), 0, groups)
    extra = jnp.where(jnp.arange(groups) == forced, MEM_GRP - 1, extra)
    order = jax.random.permutation(key_order, groups)
    before = jnp.zeros((groups,), jnp.int32).at[order].set(jnp.roll(order, 1).astype(jnp.int32))
    killed_count = extra[before]
    rotate = jax.random.randint(key_rotate, (groups,), 0, MEM_GRP - 1)
    slots = jnp.arange(MEM_GRP)
    relative = (slots[None, :] - hot_slot[:, None]) % MEM_GRP
    ranking = (relative - 1 - rotate[:, None]) % (MEM_GRP - 1)
    is_killed = (relative > 0) & (ranking < killed_count[:, None])
    is_hot = relative == 0
    counts = jnp.where(is_hot, 1 + extra[:, None], jnp.where(is_killed, 0, 1)).reshape(-1)
    donor = before * MEM_GRP + hot_slot[before]
    own_slot = jnp.arange(MEMBERS).reshape(groups, MEM_GRP)
    source = jnp.where(is_killed, donor[:, None], own_slot).reshape(-1)
    return (counts.astype(jnp.int32), source.astype(jnp.int32))


def draw_counts(key, part):
    return clone_plan(key)[0]


def draw_source(key, part):
    return clone_plan(key)[1]


def draw_mixing(key, part):
    key_diag, key_off = jax.random.split(jax.random.fold_in(key, 313))
    order_size = FLD * LEV
    diagonal = jax.random.uniform(key_diag, (order_size,), jnp.float32, 0.85, 1.0)
    offside = jax.random.uniform(key_off, (order_size, order_size), jnp.float32, -0.08, 0.08)
    identity = jnp.eye(order_size, dtype=jnp.float32)
    return offside * (1.0 - identity) + identity * diagonal[None, :]


def touch_ends(array, key, smallest, largest):
    longest = array.shape.index(max(array.shape))
    spots = []
    for shift in (0, 1):
        where = [jax.random.randint(jax.random.fold_in(key, axis), (), 0, length) for axis, length in enumerate(array.shape)]
        where[longest] = (where[longest] + shift) % array.shape[longest]
        spots.append(tuple(where))
    return array.at[spots[0]].set(smallest).at[spots[1]].set(largest)


def shard_levels(key, extent, shards, low, top_value):
    loudness, own = 1.0, jax.random.fold_in(key, 6)
    for axis_at, shards_of in shards:
        heights = jnp.exp(jax.random.uniform(jax.random.fold_in(own, axis_at), (shards_of,), jnp.float32, low / len(shards), top_value / len(shards)))
        loudness = loudness * jnp.repeat(heights, extent[axis_at] // shards_of).reshape([-1 if axis == axis_at else 1 for axis in range(len(extent))])
    return loudness


def bell_draw(own_key, dims, deviation, reach, cuts=(), kind=jnp.bfloat16):
    drawn = jax.random.normal(own_key, dims, jnp.float32) * deviation
    if len(cuts) > 0:
        drawn = shard_levels(own_key, dims, cuts, -0.22, 0.18) * drawn
    return jnp.clip(drawn, min=-reach, max=reach).astype(kind)


def setup_inputs(seed: int = 0) -> dict:
    key_of = jax.random.split(jax.random.key(seed), 10)
    fields = bell_draw(key_of[0], (MEMBERS, FLD * LEV, NLAT, NLON), 1.0, 6.0, ((0, 8), (2, 4)), jnp.float32)
    diffusion = jnp.clip(jnp.exp(math.log(0.245) - 0.7137665 * jax.random.uniform(key_of[1], (NLAT, NLON), jnp.float32) ** shard_levels(key_of[1], (NLAT, NLON), ((0, 4),), -0.2, 0.2)), 0.12, 0.245)
    mixing = draw_mixing(jax.random.fold_in(key_of[9], 71), 0)
    heating = bell_draw(key_of[3], (FLD * LEV, NLAT, NLON), 0.3, 2.0, ((1, 4),), jnp.float32)
    land_mask = touch_ends((jax.random.randint(key_of[4], (NLAT, NLON), 0, 3) < 1).astype(jnp.int32), jax.random.fold_in(key_of[4], 1), 0, 1)
    conv_weight = bell_draw(key_of[5], (CH, 27), 27 ** -0.5, 1.25, (), jnp.float32)
    head_weight = bell_draw(key_of[6], (CH, NLAT, NLON), (CH * NLAT * NLON) ** -0.5, 0.01171875, ((1, 4),), jnp.float32)
    counts = draw_counts(jax.random.fold_in(key_of[9], 71), 0)
    source = draw_source(jax.random.fold_in(key_of[9], 71), 0)
    return dict(fields=fields, diffusion=diffusion, mixing=mixing, heating=heating, land_mask=land_mask, conv_weight=conv_weight, head_weight=head_weight, counts=counts, source=source)


def advance(values, diffusion, mixing, heating):
    padded = jnp.pad(values, ((0, 0), (0, 0), (1, 1), (0, 0)))
    laplace = padded[:, :, 2:] + padded[:, :, :-2] + jnp.roll(values, 1, 3) + jnp.roll(values, -1, 3) - 4.0 * values
    smooth = values + diffusion * laplace
    mixed = jnp.einsum('ij,mjac->miac', mixing, smooth, precision=lax.Precision.HIGHEST)
    return mixed + heating - 0.05 * mixed * mixed * mixed


def surface_inputs(final, land_mask):
    land_float = land_mask.astype(jnp.float32)
    temper = final[:, 0]
    moisture = final[:, LEV]
    return jnp.stack([temper * land_float, moisture, temper * (1.0 - land_float)], 1)


def score_terms(padded, conv_weight, head_weight):
    height = padded.shape[2] - 2
    members_here = padded.shape[0]
    taps = [jnp.roll(padded[:, :, shift_lat:shift_lat + height], -shift_lon, 3) for shift_lat in range(3) for shift_lon in (-1, 0, 1)]
    patches = jnp.stack(taps, 2).reshape(members_here, 27, height * padded.shape[3])
    hidden = jax.nn.relu(jnp.einsum('ck,mkp->mcp', conv_weight, patches, precision=lax.Precision.HIGHEST))
    return jnp.einsum('mcp,cp->m', hidden, head_weight.reshape(head_weight.shape[0], -1), precision=lax.Precision.HIGHEST)


def reference(fields, diffusion, mixing, heating, land_mask, conv_weight, head_weight, counts, source):
    final = fields
    for repeat in range(STEPS):
        final = advance(final, diffusion, mixing, heating)
    inputs = surface_inputs(final, land_mask)
    padded = jnp.pad(inputs, ((0, 0), (0, 0), (1, 1), (0, 0)))
    scores = score_terms(padded, conv_weight, head_weight)
    weights = jnp.exp(scores)
    weights = weights / jnp.mean(weights)
    new_fields = final[source]
    slot_weight = weights[source] / counts[source].astype(jnp.float32)
    return new_fields, scores, slot_weight
```

```python
import functools
import jax
import jax.numpy as jnp
from jax import lax
from jax.experimental import pallas as pl
from jax.experimental.pallas import tpu as pltpu
from jax.sharding import PartitionSpec as P

LEV = 10
STEPS = 4
SUB = 8
CHUNKS = 4
EXT = 2 * STEPS
F32 = jnp.float32
BF16 = jnp.bfloat16


def split_hi_lo(value):
    hi = value.astype(BF16)
    lo = (value - hi.astype(F32)).astype(BF16)
    return hi, lo


def split_constant(value):
    hi = lax.reduce_precision(value, 8, 7)
    return hi.astype(BF16), (value - hi).astype(BF16)


def dot3(a_hi, a_lo, b_hi, b_lo):
    dot = functools.partial(jnp.dot, preferred_element_type=F32)
    return dot(a_hi, b_hi) + (dot(a_hi, b_lo) + dot(a_lo, b_hi))


def steps_body(fields_ref, below_ref, above_ref, diff_ref, heat_ref, w_hi_ref, w_lo_ref, x_ref, y_hi_ref, y_lo_ref):
    members, levels, rows, lon = x_ref.shape
    own = rows - EXT
    tiles = rows // SUB
    width = members * tiles * lon
    cols = min(2 * lon, width)
    x_ref[:, :, :own, :] = fields_ref[...]
    x_ref[:, :, own : own + STEPS, :] = below_ref[...]
    x_ref[:, :, own + STEPS :, :] = above_ref[...]
    place = lax.broadcasted_iota(jnp.int32, (1, SUB, lon), 1)
    depth = jnp.where(place < STEPS, place, SUB - 1 - place)

    def one_step(step, carry):
        for g in range(members):
            for f in range(0, levels, 2):
                x = x_ref[g, f : f + 2]
                near = (
                    pltpu.roll(x, 1, 1)
                    + pltpu.roll(x, rows - 1, 1)
                    + pltpu.roll(x, 1, 2)
                    + pltpu.roll(x, lon - 1, 2)
                    - 4.0 * x
                )
                y = x + diff_ref[...][None] * near
                for t in range(tiles):
                    part = y[:, SUB * t : SUB * (t + 1), :].reshape(2 * SUB, lon)
                    hi, lo = split_hi_lo(part)
                    at = (g * tiles + t) * lon
                    y_hi_ref[SUB * f : SUB * (f + 2), at : at + lon] = hi
                    y_lo_ref[SUB * f : SUB * (f + 2), at : at + lon] = lo
        for start in range(0, width, cols):
            end = min(start + cols, width)
            z = dot3(w_hi_ref[...], w_lo_ref[...], y_hi_ref[:, start:end], y_lo_ref[:, start:end])
            for at in range(start, end, lon):
                g, t = divmod(at // lon, tiles)
                mixed = z[:, at - start : at - start + lon].reshape(levels, SUB, lon)
                new = mixed + heat_ref[:, SUB * t : SUB * (t + 1), :] - 0.05 * mixed * mixed * mixed
                if t == tiles - 1:
                    new = jnp.where(depth < STEPS - 1 - step, new, 0.0)
                x_ref[g, :, SUB * t : SUB * (t + 1), :] = new
        return carry

    lax.fori_loop(0, STEPS, one_step, 0)


def donor_kernel(fields_ref, below_ref, above_ref, diff_ref, heat_ref, w_hi_ref, w_lo_ref, out_ref, x_ref, y_hi_ref, y_lo_ref):
    steps_body(fields_ref, below_ref, above_ref, diff_ref, heat_ref, w_hi_ref, w_lo_ref, x_ref, y_hi_ref, y_lo_ref)
    out_ref[...] = x_ref[:, :, : out_ref.shape[2], :]


def chunk_kernel(first, killed_ref, fields_ref, below_ref, above_ref, donor_ref, diff_ref, heat_ref, w_hi_ref, w_lo_ref, *rest):
    out_ref, tq_ref, x_ref, y_hi_ref, y_lo_ref = rest[-5:]
    steps_body(fields_ref, below_ref, above_ref, diff_ref, heat_ref, w_hi_ref, w_lo_ref, x_ref, y_hi_ref, y_lo_ref)
    members, levels, own, lon = out_ref.shape
    for g in range(members):
        tq_ref[g, 0] = x_ref[g, 0, :own, :]
        tq_ref[g, 1] = x_ref[g, LEV, :own, :]
        killed = killed_ref[first + pl.program_id(0) * members + g] != 0

        @pl.when(killed)
        def _():
            out_ref[g] = donor_ref[0]

        @pl.when(jnp.logical_not(killed))
        def _():
            out_ref[g] = x_ref[g, :, :own, :]


def score_kernel(tq_ref, ext_ref, land_ref, b_hi_ref, b_lo_ref, head_ref, out_ref):
    members, _, own, lon = tq_ref.shape
    land = land_ref[...]
    depth = b_hi_ref.shape[1]
    pad = depth - 9 * (own + SUB)
    highs, lows = [], []
    for g in range(members):
        t = jnp.concatenate([tq_ref[g, 0], ext_ref[g, 0]], axis=0)
        q = jnp.concatenate([tq_ref[g, 1], ext_ref[g, 1]], axis=0)
        rows = []
        for value in (t * land, q, t * (1.0 - land)):
            rows += [pltpu.roll(value, 1, 1), value, pltpu.roll(value, lon - 1, 1)]
        if pad:
            rows.append(jnp.zeros((pad, lon), F32))
        hi, lo = split_hi_lo(jnp.concatenate(rows, axis=0))
        highs.append(hi)
        lows.append(lo)
    for g in range(0, members, 2):
        hidden = dot3(
            b_hi_ref[...],
            b_lo_ref[...],
            jnp.concatenate(highs[g : g + 2], axis=1),
            jnp.concatenate(lows[g : g + 2], axis=1),
        )
        hidden = jnp.maximum(hidden, 0.0)
        for k in range(2):
            terms = hidden[:, k * lon : (k + 1) * lon] * head_ref[...]
            out_ref[g + k : g + k + 1, :] = jnp.sum(terms, axis=0, keepdims=True)


def params():
    return pltpu.CompilerParams(vmem_limit_bytes=40 * 2**20)


def full_spec(array):
    zeros = (0,) * array.ndim
    return pl.BlockSpec(array.shape, lambda *_: zeros)


def steps_scratch(members, levels, rows, lon):
    width = members * (rows // SUB) * lon
    return [
        pltpu.VMEM((members, levels, rows, lon), F32),
        pltpu.VMEM((levels * SUB, width), BF16),
        pltpu.VMEM((levels * SUB, width), BF16),
    ]


def run_donor(donor, below, above, consts):
    _, levels, own, lon = donor.shape
    ins = (donor, below, above) + consts
    return pl.pallas_call(
        donor_kernel,
        out_shape=jax.ShapeDtypeStruct(donor.shape, F32),
        in_specs=[full_spec(a) for a in ins],
        out_specs=full_spec(donor),
        grid=(1,),
        scratch_shapes=steps_scratch(1, levels, own + EXT, lon),
        compiler_params=params(),
        name="donor_steps",
    )(*ins)


def run_chunk(index, size, killed, fields, below, above, donor, consts, held):
    members, levels, own, lon = fields.shape
    group = 2
    blocks = size // group
    first = index * size
    block = pl.BlockSpec((group, levels, own, lon), lambda i: (i + index * blocks, 0, 0, 0))
    halo = pl.BlockSpec((group, levels, STEPS, lon), lambda i: (i, 0, 0, 0))
    ins = [killed, fields, below, above, donor, *consts]
    in_specs = [pl.BlockSpec(memory_space=pltpu.SMEM), block, halo, halo, full_spec(donor)]
    in_specs += [full_spec(a) for a in consts]
    alias = {}
    if held is not None:
        alias = {len(ins): 0}
        ins.append(held)
        in_specs.append(pl.BlockSpec(memory_space=pl.ANY))
    flops = 6 * size * levels * levels * SUB * (own + EXT) * lon * STEPS
    return pl.pallas_call(
        functools.partial(chunk_kernel, first),
        out_shape=(
            jax.ShapeDtypeStruct(fields.shape, F32),
            jax.ShapeDtypeStruct((size, 2, own, lon), F32),
        ),
        in_specs=in_specs,
        out_specs=(block, pl.BlockSpec((group, 2, own, lon), lambda i: (i, 0, 0, 0))),
        grid=(blocks,),
        scratch_shapes=steps_scratch(group, levels, own + EXT, lon),
        input_output_aliases=alias,
        compiler_params=params(),
        cost_estimate=pl.CostEstimate(flops=flops, bytes_accessed=2 * size * levels * own * lon * 4, transcendentals=0),
        name="chunk_steps",
    )(*ins)


def run_scores(tq, ext, land, b_hi, b_lo, head):
    members, _, own, lon = tq.shape
    group = 8
    return pl.pallas_call(
        score_kernel,
        out_shape=jax.ShapeDtypeStruct((members, lon), F32),
        in_specs=[
            pl.BlockSpec((group, 2, own, lon), lambda i: (i, 0, 0, 0)),
            pl.BlockSpec((group, 2, SUB, lon), lambda i: (i, 0, 0, 0)),
            full_spec(land),
            full_spec(b_hi),
            full_spec(b_lo),
            full_spec(head),
        ],
        out_specs=pl.BlockSpec((group, lon), lambda i: (i, 0)),
        grid=(members // group,),
        compiler_params=params(),
        name="score_terms",
    )(tq, ext, land, b_hi, b_lo, head)


def halos(value, dim, width, axis="lat"):
    size, length = lax.axis_size(axis), value.shape[dim]
    up = [(i, i + 1) for i in range(size - 1)]
    down = [(j, i) for i, j in up]
    above = lax.ppermute(lax.slice_in_dim(value, length - width, length, axis=dim), axis, up)
    below = lax.ppermute(lax.slice_in_dim(value, 0, width, axis=dim), axis, down)
    return below, above


def conv_matrix(conv_weight, own):
    rows = own + SUB
    channels = conv_weight.shape[0]
    taps = conv_weight.reshape(channels, 1, 3, 3, 3, 1)
    i = jnp.arange(own)[:, None, None]
    a = jnp.arange(3)[None, :, None]
    r = jnp.arange(rows)[None, None, :]
    hit = ((i + a - 1) % rows == r).astype(F32)
    parts = [taps[:, :, :, k] * hit[None, :, None, None, k, :] for k in range(3)]
    matrix = (parts[0] + parts[1] + parts[2]).reshape(channels * own, 9 * rows)
    pad = -matrix.shape[1] % 16
    return jnp.pad(matrix, ((0, 0), (0, pad)))


def local(fields, diffusion, mixing, heating, land_mask, conv_weight, head_weight, counts, source):
    members, levels, own, lon = fields.shape
    total_members = counts.shape[0]
    me = lax.axis_index("grp")
    offset = me * members
    local_counts = lax.dynamic_slice_in_dim(counts, offset, members)
    local_source = lax.dynamic_slice_in_dim(source, offset, members)
    killed = (local_source != offset + jnp.arange(members, dtype=jnp.int32)).astype(jnp.int32)
    donor_group = jnp.max(jnp.where(killed > 0, local_source // members, 0))

    hot = lax.dynamic_index_in_dim(fields, jnp.argmax(local_counts), 0, keepdims=False)
    hot_all = jnp.concatenate([hot, *halos(hot, 1, STEPS)], axis=1)
    gathered = lax.all_gather(hot_all, "grp", axis=0)
    donor_all = lax.dynamic_index_in_dim(gathered, donor_group, 0, keepdims=True)

    diff_all = jnp.concatenate([diffusion, *halos(diffusion, 0, STEPS)], axis=0)
    heat_all = jnp.concatenate([heating, *halos(heating, 1, STEPS)], axis=1)
    eye = jnp.eye(SUB, dtype=F32)
    wide = (mixing[:, None, :, None] * eye[None, :, None, :]).reshape(levels * SUB, levels * SUB)
    consts = (diff_all, heat_all, *split_constant(wide))

    donor = run_donor(
        donor_all[:, :, :own],
        donor_all[:, :, own : own + STEPS],
        donor_all[:, :, own + STEPS :],
        consts,
    )
    size = members // CHUNKS
    held, parts = None, []
    for c in range(CHUNKS):
        piece = lax.slice_in_dim(fields, c * size, (c + 1) * size, axis=0)
        below, above = halos(piece, 2, STEPS)
        held, tq = run_chunk(c, size, killed, fields, below, above, donor, consts, held)
        parts.append(tq)
    tq = jnp.concatenate(parts, axis=0)

    land = land_mask.astype(F32)
    land_below, land_above = halos(land, 0, 1)
    land_all = jnp.concatenate([land, land_below, jnp.zeros((SUB - 2, lon), F32), land_above], axis=0)
    tq_below, tq_above = halos(tq, 2, 1)
    ext = jnp.concatenate([tq_below, jnp.zeros((members, 2, SUB - 2, lon), F32), tq_above], axis=2)
    b_hi, b_lo = split_constant(conv_matrix(conv_weight, own))
    partial = run_scores(tq, ext, land_all, b_hi, b_lo, head_weight.reshape(-1, lon))
    partial = jnp.sum(partial, axis=1)
    everything = lax.all_gather(partial, ("lat", "grp"), axis=0)
    all_scores = everything.reshape(lax.axis_size("lat"), total_members).sum(0)
    scores = lax.dynamic_slice_in_dim(all_scores, offset, members)
    weights = jnp.exp(all_scores)
    weights = weights / jnp.mean(weights)
    selector = (local_source[:, None] == jnp.arange(total_members, dtype=jnp.int32)[None, :]).astype(F32)
    chosen_weight = jnp.sum(selector * weights[None, :], 1)
    chosen_count = jnp.sum(selector * counts.astype(F32)[None, :], 1)
    return held, scores, chosen_weight / chosen_count


def solution(mesh):
    return jax.shard_map(
        local,
        mesh=mesh,
        in_specs=(
            P("grp", None, "lat", None),
            P("lat", None),
            P(),
            P(None, "lat", None),
            P("lat", None),
            P(),
            P(None, "lat", None),
            P(),
            P(),
        ),
        out_specs=(P("grp", None, "lat", None), P("grp"), P("grp")),
        check_vma=False,
    )
```

```python
import functools
import jax
import jax.numpy as jnp
from jax import lax
from jax.experimental import pallas as pl
from jax.experimental.pallas import tpu as pltpu
from jax.sharding import PartitionSpec as P

LEV = 10
STEPS = 4
SUB = 8
CHUNKS = 4
EXT = 2 * STEPS
F32 = jnp.float32
BF16 = jnp.bfloat16


def split_hi_lo(value):
    hi = value.astype(BF16)
    lo = (value - hi.astype(F32)).astype(BF16)
    return hi, lo


def split_constant(value):
    hi = lax.reduce_precision(value, 8, 7)
    return hi.astype(BF16), (value - hi).astype(BF16)


def dot3(a_hi, a_lo, b_hi, b_lo):
    dot = functools.partial(jnp.dot, preferred_element_type=F32)
    return dot(a_hi, b_hi) + (dot(a_hi, b_lo) + dot(a_lo, b_hi))


def steps_body(fields_ref, below_ref, above_ref, diff_ref, heat_ref, w_hi_ref, w_lo_ref, x_ref, y_hi_ref, y_lo_ref):
    members, levels, rows, lon = x_ref.shape
    own = rows - EXT
    tiles = rows // SUB
    width = members * tiles * lon
    cols = min(2 * lon, width)
    x_ref[:, :, :own, :] = fields_ref[...]
    x_ref[:, :, own : own + STEPS, :] = below_ref[...]
    x_ref[:, :, own + STEPS :, :] = above_ref[...]
    place = lax.broadcasted_iota(jnp.int32, (1, SUB, lon), 1)
    depth = jnp.where(place < STEPS, place, SUB - 1 - place)

    def one_step(step, carry):
        for g in range(members):
            for f in range(0, levels, 2):
                x = x_ref[g, f : f + 2]
                near = (
                    pltpu.roll(x, 1, 1)
                    + pltpu.roll(x, rows - 1, 1)
                    + pltpu.roll(x, 1, 2)
                    + pltpu.roll(x, lon - 1, 2)
                    - 4.0 * x
                )
                y = x + diff_ref[...][None] * near
                for t in range(tiles):
                    part = y[:, SUB * t : SUB * (t + 1), :].reshape(2 * SUB, lon)
                    hi, lo = split_hi_lo(part)
                    at = (g * tiles + t) * lon
                    y_hi_ref[SUB * f : SUB * (f + 2), at : at + lon] = hi
                    y_lo_ref[SUB * f : SUB * (f + 2), at : at + lon] = lo
        for start in range(0, width, cols):
            end = min(start + cols, width)
            z = dot3(w_hi_ref[...], w_lo_ref[...], y_hi_ref[:, start:end], y_lo_ref[:, start:end])
            for at in range(start, end, lon):
                g, t = divmod(at // lon, tiles)
                mixed = z[:, at - start : at - start + lon].reshape(levels, SUB, lon)
                new = mixed + heat_ref[:, SUB * t : SUB * (t + 1), :] - 0.05 * mixed * mixed * mixed
                if t == tiles - 1:
                    new = jnp.where(depth < STEPS - 1 - step, new, 0.0)
                x_ref[g, :, SUB * t : SUB * (t + 1), :] = new
        return carry

    lax.fori_loop(0, STEPS, one_step, 0)


def donor_kernel(fields_ref, below_ref, above_ref, diff_ref, heat_ref, w_hi_ref, w_lo_ref, out_ref, x_ref, y_hi_ref, y_lo_ref):
    steps_body(fields_ref, below_ref, above_ref, diff_ref, heat_ref, w_hi_ref, w_lo_ref, x_ref, y_hi_ref, y_lo_ref)
    out_ref[...] = x_ref[:, :, : out_ref.shape[2], :]


def chunk_kernel(first, killed_ref, fields_ref, below_ref, above_ref, donor_ref, diff_ref, heat_ref, w_hi_ref, w_lo_ref, *rest):
    out_ref, tq_ref, x_ref, y_hi_ref, y_lo_ref = rest[-5:]
    steps_body(fields_ref, below_ref, above_ref, diff_ref, heat_ref, w_hi_ref, w_lo_ref, x_ref, y_hi_ref, y_lo_ref)
    members, levels, own, lon = out_ref.shape
    for g in range(members):
        tq_ref[g, 0] = x_ref[g, 0, :own, :]
        tq_ref[g, 1] = x_ref[g, LEV, :own, :]
        killed = killed_ref[first + pl.program_id(0) * members + g] != 0

        @pl.when(killed)
        def _():
            out_ref[g] = donor_ref[0]

        @pl.when(jnp.logical_not(killed))
        def _():
            out_ref[g] = x_ref[g, :, :own, :]


def peers(axis, send):
    size = lax.axis_size(axis)
    me = lax.axis_index(axis)
    for d in range(1, size):
        send(lax.rem(me + d, size), d)


def exchange(axis, mine_ref, slots_ref, send_sem, recv_sem):
    me = lax.axis_index(axis)

    def copy(other, slot, d):
        return pltpu.make_async_remote_copy(
            src_ref=mine_ref,
            dst_ref=slots_ref.at[slot],
            send_sem=send_sem.at[d],
            recv_sem=recv_sem.at[slot],
            device_id={axis: other},
            device_id_type=pl.DeviceIdType.MESH,
        )

    peers(axis, lambda other, d: copy(other, me, d).start())
    slots_ref[me] = mine_ref[...]
    peers(axis, lambda other, d: copy(other, other, d).wait_recv())
    peers(axis, lambda other, d: copy(other, me, d).wait_send())


def greet():
    barrier = pltpu.get_barrier_semaphore()
    for axis in ("lat", "grp"):
        peers(
            axis,
            lambda other, d: pl.semaphore_signal(
                barrier, inc=1, device_id={axis: other}, device_id_type=pl.DeviceIdType.MESH
            ),
        )
    pl.semaphore_wait(barrier, lax.axis_size("lat") + lax.axis_size("grp") - 2)


def finish_kernel(
    tq_ref, land_ref, b_hi_ref, b_lo_ref, head_ref, out_ref,
    first_ref, last_ref, below_ref, above_ref, part_ref, mine_ref, lat_slots, sum_ref, grp_slots,
    edge_send, edge_recv, lat_send, lat_recv, grp_send, grp_recv,
):
    members, _, own, lon = tq_ref.shape
    me, size = lax.axis_index("lat"), lax.axis_size("lat")
    for m in range(members):
        for k in range(2):
            at = 2 * m + k
            first_ref[at : at + 1, :] = tq_ref[m, k, 0:1, :]
            last_ref[at : at + 1, :] = tq_ref[m, k, own - 1 : own, :]
    greet()

    def edge(way, other):
        return pltpu.make_async_remote_copy(
            src_ref=(first_ref, last_ref)[way],
            dst_ref=(below_ref, above_ref)[way],
            send_sem=edge_send.at[way],
            recv_sem=edge_recv.at[way],
            device_id={"lat": other},
            device_id_type=pl.DeviceIdType.MESH,
        )

    @pl.when(me > 0)
    def _():
        edge(0, me - 1).start()

    @pl.when(me < size - 1)
    def _():
        edge(1, me + 1).start()

    @pl.when(me > 0)
    def _():
        edge(1, me - 1).wait_recv()
        edge(0, me - 1).wait_send()

    @pl.when(me < size - 1)
    def _():
        edge(0, me + 1).wait_recv()
        edge(1, me + 1).wait_send()

    @pl.when(me == 0)
    def _():
        above_ref[...] = jnp.zeros_like(above_ref)

    @pl.when(me == size - 1)
    def _():
        below_ref[...] = jnp.zeros_like(below_ref)

    land = land_ref[...]
    pad = b_hi_ref.shape[1] - 9 * (own + SUB)
    place = lax.broadcasted_iota(jnp.int32, (SUB, lon), 0)

    def pair(i, carry):
        highs, lows = [], []
        for g in range(2):
            values = []
            for k in range(2):
                at = 4 * i + 2 * g + k
                ext = jnp.where(
                    place == 0,
                    below_ref[pl.ds(at, 1), :],
                    jnp.where(place == SUB - 1, above_ref[pl.ds(at, 1), :], 0.0),
                )
                values.append(jnp.concatenate([tq_ref[2 * i + g, k], ext], axis=0))
            t, q = values
            rows = []
            for value in (t * land, q, t * (1.0 - land)):
                rows += [pltpu.roll(value, 1, 1), value, pltpu.roll(value, lon - 1, 1)]
            if pad:
                rows.append(jnp.zeros((pad, lon), F32))
            hi, lo = split_hi_lo(jnp.concatenate(rows, axis=0))
            highs.append(hi)
            lows.append(lo)
        hidden = dot3(
            b_hi_ref[...], b_lo_ref[...], jnp.concatenate(highs, axis=1), jnp.concatenate(lows, axis=1)
        )
        hidden = jnp.maximum(hidden, 0.0)
        for g in range(2):
            terms = hidden[:, g * lon : (g + 1) * lon] * head_ref[...]
            part_ref[pl.ds(2 * i + g, 1), :] = jnp.sum(terms, axis=0, keepdims=True)
        return carry

    lax.fori_loop(0, members // 2, pair, 0)
    total = jnp.sum(part_ref[...], axis=1, keepdims=True)
    row = lax.broadcasted_iota(jnp.int32, (members, lon), 0)
    col = lax.broadcasted_iota(jnp.int32, (members, lon), 1)
    flat = jnp.sum(jnp.where(row == col, total, 0.0), axis=0, keepdims=True)
    mine_ref[...] = jnp.broadcast_to(flat, mine_ref.shape)
    exchange("lat", mine_ref, lat_slots, lat_send, lat_recv)
    score = lat_slots[0]
    for k in range(1, size):
        score = score + lat_slots[k]
    sum_ref[...] = score
    exchange("grp", sum_ref, grp_slots, grp_send, grp_recv)
    out_ref[...] = grp_slots[...]


def params():
    return pltpu.CompilerParams(vmem_limit_bytes=40 * 2**20)


def full_spec(array):
    zeros = (0,) * array.ndim
    return pl.BlockSpec(array.shape, lambda *_: zeros)


def steps_scratch(members, levels, rows, lon):
    width = members * (rows // SUB) * lon
    return [
        pltpu.VMEM((members, levels, rows, lon), F32),
        pltpu.VMEM((levels * SUB, width), BF16),
        pltpu.VMEM((levels * SUB, width), BF16),
    ]


def run_donor(donor, below, above, consts):
    _, levels, own, lon = donor.shape
    ins = (donor, below, above) + consts
    return pl.pallas_call(
        donor_kernel,
        out_shape=jax.ShapeDtypeStruct(donor.shape, F32),
        in_specs=[full_spec(a) for a in ins],
        out_specs=full_spec(donor),
        grid=(1,),
        scratch_shapes=steps_scratch(1, levels, own + EXT, lon),
        compiler_params=params(),
        name="donor_steps",
    )(*ins)


def run_chunk(index, size, killed, fields, below, above, donor, consts, held):
    members, levels, own, lon = fields.shape
    group = 2
    blocks = size // group
    first = index * size
    block = pl.BlockSpec((group, levels, own, lon), lambda i: (i + index * blocks, 0, 0, 0))
    halo = pl.BlockSpec((group, levels, STEPS, lon), lambda i: (i, 0, 0, 0))
    ins = [killed, fields, below, above, donor, *consts]
    in_specs = [pl.BlockSpec(memory_space=pltpu.SMEM), block, halo, halo, full_spec(donor)]
    in_specs += [full_spec(a) for a in consts]
    alias = {}
    if held is not None:
        alias = {len(ins): 0}
        ins.append(held)
        in_specs.append(pl.BlockSpec(memory_space=pl.ANY))
    flops = 6 * size * levels * levels * SUB * (own + EXT) * lon * STEPS
    return pl.pallas_call(
        functools.partial(chunk_kernel, first),
        out_shape=(
            jax.ShapeDtypeStruct(fields.shape, F32),
            jax.ShapeDtypeStruct((size, 2, own, lon), F32),
        ),
        in_specs=in_specs,
        out_specs=(block, pl.BlockSpec((group, 2, own, lon), lambda i: (i, 0, 0, 0))),
        grid=(blocks,),
        scratch_shapes=steps_scratch(group, levels, own + EXT, lon),
        input_output_aliases=alias,
        compiler_params=params(),
        cost_estimate=pl.CostEstimate(flops=flops, bytes_accessed=2 * size * levels * own * lon * 4, transcendentals=0),
        name="chunk_steps",
    )(*ins)


def run_finish(tq, land, b_hi, b_lo, head):
    members, _, own, lon = tq.shape
    lat, grp = lax.axis_size("lat"), lax.axis_size("grp")
    edge = pltpu.VMEM((2 * members, lon), F32)
    tile = pltpu.VMEM((SUB, lon), F32)
    return pl.pallas_call(
        finish_kernel,
        out_shape=jax.ShapeDtypeStruct((grp, SUB, lon), F32),
        in_specs=[pl.BlockSpec(memory_space=pltpu.VMEM)] * 5,
        out_specs=pl.BlockSpec(memory_space=pltpu.VMEM),
        scratch_shapes=[
            edge, edge, edge, edge,
            pltpu.VMEM((members, lon), F32),
            tile,
            pltpu.VMEM((lat, SUB, lon), F32),
            tile,
            pltpu.VMEM((grp, SUB, lon), F32),
            pltpu.SemaphoreType.DMA((2,)),
            pltpu.SemaphoreType.DMA((2,)),
            pltpu.SemaphoreType.DMA((lat,)),
            pltpu.SemaphoreType.DMA((lat,)),
            pltpu.SemaphoreType.DMA((grp,)),
            pltpu.SemaphoreType.DMA((grp,)),
        ],
        compiler_params=pltpu.CompilerParams(
            collective_id=0, has_side_effects=True, vmem_limit_bytes=40 * 2**20
        ),
        name="finish",
    )(tq, land, b_hi, b_lo, head)


def halos(value, dim, width, axis="lat"):
    size, length = lax.axis_size(axis), value.shape[dim]
    up = [(i, i + 1) for i in range(size - 1)]
    down = [(j, i) for i, j in up]
    above = lax.ppermute(lax.slice_in_dim(value, length - width, length, axis=dim), axis, up)
    below = lax.ppermute(lax.slice_in_dim(value, 0, width, axis=dim), axis, down)
    return below, above


def conv_matrix(conv_weight, own):
    rows = own + SUB
    channels = conv_weight.shape[0]
    taps = conv_weight.reshape(channels, 1, 3, 3, 3, 1)
    i = jnp.arange(own)[:, None, None]
    a = jnp.arange(3)[None, :, None]
    r = jnp.arange(rows)[None, None, :]
    hit = ((i + a - 1) % rows == r).astype(F32)
    parts = [taps[:, :, :, k] * hit[None, :, None, None, k, :] for k in range(3)]
    matrix = (parts[0] + parts[1] + parts[2]).reshape(channels * own, 9 * rows)
    pad = -matrix.shape[1] % 16
    return jnp.pad(matrix, ((0, 0), (0, pad)))


def local(fields, diffusion, mixing, heating, land_mask, conv_weight, head_weight, counts, source):
    members, levels, own, lon = fields.shape
    total_members = counts.shape[0]
    me = lax.axis_index("grp")
    offset = me * members
    local_counts = lax.dynamic_slice_in_dim(counts, offset, members)
    local_source = lax.dynamic_slice_in_dim(source, offset, members)
    killed = (local_source != offset + jnp.arange(members, dtype=jnp.int32)).astype(jnp.int32)
    donor_group = jnp.max(jnp.where(killed > 0, local_source // members, 0))

    land = land_mask.astype(F32)
    hot = lax.dynamic_index_in_dim(fields, jnp.argmax(local_counts), 0, keepdims=False)
    stack = jnp.concatenate([hot, heating, diffusion[None], land[None]], axis=0)
    stack_all = jnp.concatenate([stack, *halos(stack, 1, STEPS)], axis=1)
    hot_all, heat_all = stack_all[:levels], stack_all[levels : 2 * levels]
    diff_all, land_all = stack_all[2 * levels], stack_all[2 * levels + 1]
    gathered = lax.all_gather(hot_all, "grp", axis=0)
    donor_all = lax.dynamic_index_in_dim(gathered, donor_group, 0, keepdims=True)
    eye = jnp.eye(SUB, dtype=F32)
    wide = (mixing[:, None, :, None] * eye[None, :, None, :]).reshape(levels * SUB, levels * SUB)
    consts = (diff_all, heat_all, *split_constant(wide))

    donor = run_donor(
        donor_all[:, :, :own],
        donor_all[:, :, own : own + STEPS],
        donor_all[:, :, own + STEPS :],
        consts,
    )
    size = members // CHUNKS
    held, parts = None, []
    for c in range(CHUNKS):
        piece = lax.slice_in_dim(fields, c * size, (c + 1) * size, axis=0)
        below, above = halos(piece, 2, STEPS)
        held, tq = run_chunk(c, size, killed, fields, below, above, donor, consts, held)
        parts.append(tq)
    tq = jnp.concatenate(parts, axis=0)

    b_hi, b_lo = split_constant(conv_matrix(conv_weight, own))
    table = run_finish(tq, land_all, b_hi, b_lo, head_weight.reshape(-1, lon))
    all_scores = table[:, 0, :members].reshape(total_members)
    scores = lax.dynamic_slice_in_dim(all_scores, offset, members)
    weights = jnp.exp(all_scores)
    weights = weights / jnp.mean(weights)
    selector = (local_source[:, None] == jnp.arange(total_members, dtype=jnp.int32)[None, :]).astype(F32)
    chosen_weight = jnp.sum(selector * weights[None, :], 1)
    chosen_count = jnp.sum(selector * counts.astype(F32)[None, :], 1)
    return held, scores, chosen_weight / chosen_count


def solution(mesh):
    return jax.shard_map(
        local,
        mesh=mesh,
        in_specs=(
            P("grp", None, "lat", None),
            P("lat", None),
            P(),
            P(None, "lat", None),
            P("lat", None),
            P(),
            P(None, "lat", None),
            P(),
            P(),
        ),
        out_specs=(P("grp", None, "lat", None), P("grp"), P("grp")),
        check_vma=False,
    )
```

```python
import functools
import jax
import jax.numpy as jnp
from jax import lax
from jax.experimental import pallas as pl
from jax.experimental.pallas import tpu as pltpu
from jax.sharding import PartitionSpec as P

LEV = 10
STEPS = 4
SUB = 8
CHUNKS = 8
EXT = 2 * STEPS
F32 = jnp.float32
BF16 = jnp.bfloat16


def split_hi_lo(value):
    hi = value.astype(BF16)
    lo = (value - hi.astype(F32)).astype(BF16)
    return hi, lo


def split_constant(value):
    hi = lax.reduce_precision(value, 8, 7)
    return hi.astype(BF16), (value - hi).astype(BF16)


def dot3(a_hi, a_lo, b_hi, b_lo):
    dot = functools.partial(jnp.dot, preferred_element_type=F32)
    return dot(a_hi, b_hi) + (dot(a_hi, b_lo) + dot(a_lo, b_hi))


def steps_body(fields_ref, below_ref, above_ref, diff_ref, heat_ref, w_hi_ref, w_lo_ref, x_ref, y_hi_ref, y_lo_ref):
    members, levels, rows, lon = x_ref.shape
    own = rows - EXT
    tiles = rows // SUB
    width = members * tiles * lon
    cols = min(2 * lon, width)
    x_ref[:, :, :own, :] = fields_ref[...]
    x_ref[:, :, own : own + STEPS, :] = below_ref[...]
    x_ref[:, :, own + STEPS :, :] = above_ref[...]
    place = lax.broadcasted_iota(jnp.int32, (1, SUB, lon), 1)
    depth = jnp.where(place < STEPS, place, SUB - 1 - place)

    def one_step(step, carry):
        for g in range(members):
            for f in range(0, levels, 2):
                x = x_ref[g, f : f + 2]
                near = (
                    pltpu.roll(x, 1, 1)
                    + pltpu.roll(x, rows - 1, 1)
                    + pltpu.roll(x, 1, 2)
                    + pltpu.roll(x, lon - 1, 2)
                    - 4.0 * x
                )
                y = x + diff_ref[...][None] * near
                for t in range(tiles):
                    part = y[:, SUB * t : SUB * (t + 1), :].reshape(2 * SUB, lon)
                    hi, lo = split_hi_lo(part)
                    at = (g * tiles + t) * lon
                    y_hi_ref[SUB * f : SUB * (f + 2), at : at + lon] = hi
                    y_lo_ref[SUB * f : SUB * (f + 2), at : at + lon] = lo
        for start in range(0, width, cols):
            end = min(start + cols, width)
            z = dot3(w_hi_ref[...], w_lo_ref[...], y_hi_ref[:, start:end], y_lo_ref[:, start:end])
            for at in range(start, end, lon):
                g, t = divmod(at // lon, tiles)
                mixed = z[:, at - start : at - start + lon].reshape(levels, SUB, lon)
                new = mixed + heat_ref[:, SUB * t : SUB * (t + 1), :] - 0.05 * mixed * mixed * mixed
                if t == tiles - 1:
                    new = jnp.where(depth < STEPS - 1 - step, new, 0.0)
                x_ref[g, :, SUB * t : SUB * (t + 1), :] = new
        return carry

    lax.fori_loop(0, STEPS, one_step, 0)


def donor_kernel(fields_ref, below_ref, above_ref, diff_ref, heat_ref, w_hi_ref, w_lo_ref, out_ref, x_ref, y_hi_ref, y_lo_ref):
    steps_body(fields_ref, below_ref, above_ref, diff_ref, heat_ref, w_hi_ref, w_lo_ref, x_ref, y_hi_ref, y_lo_ref)
    out_ref[...] = x_ref[:, :, : out_ref.shape[2], :]


def main_kernel(
    fields_ref, low_ref, high_ref, diff_ref, heat_ref, w_hi_ref, w_lo_ref, out_ref, tq_ref,
    below_ref, above_ref, x_ref, y_hi_ref, y_lo_ref, send_sem, recv_sem,
):
    members, levels, own, lon = out_ref.shape
    group = x_ref.shape[0]
    size = members // CHUNKS
    me, bands = lax.axis_index("lat"), lax.axis_size("lat")

    def halo(way, chunk, other):
        part = pl.ds(chunk * size, size)
        return pltpu.make_async_remote_copy(
            src_ref=(low_ref, high_ref)[way].at[part],
            dst_ref=(below_ref, above_ref)[way].at[part],
            send_sem=send_sem.at[way, chunk],
            recv_sem=recv_sem.at[way, chunk],
            device_id={"lat": other},
            device_id_type=pl.DeviceIdType.MESH,
        )

    greet(("lat",))

    def begin(chunk, carry):
        @pl.when(me > 0)
        def _():
            halo(0, chunk, me - 1).start()

        @pl.when(me < bands - 1)
        def _():
            halo(1, chunk, me + 1).start()

        return carry

    lax.fori_loop(0, CHUNKS, begin, 0)

    @pl.when(me == 0)
    def _():
        above_ref[...] = jnp.zeros_like(above_ref)

    @pl.when(me == bands - 1)
    def _():
        below_ref[...] = jnp.zeros_like(below_ref)

    def work(chunk, carry):
        @pl.when(me > 0)
        def _():
            halo(1, chunk, me - 1).wait_recv()

        @pl.when(me < bands - 1)
        def _():
            halo(0, chunk, me + 1).wait_recv()

        def few(i, inner):
            part = pl.ds(chunk * size + i * group, group)
            steps_body(
                fields_ref.at[part], below_ref.at[part], above_ref.at[part],
                diff_ref, heat_ref, w_hi_ref, w_lo_ref, x_ref, y_hi_ref, y_lo_ref,
            )
            out_ref[part] = x_ref[:, :, :own, :]
            tq_ref[part, 0] = x_ref[:, 0, :own, :]
            tq_ref[part, 1] = x_ref[:, LEV, :own, :]
            return inner

        lax.fori_loop(0, size // group, few, 0)
        return carry

    lax.fori_loop(0, CHUNKS, work, 0)

    def end(chunk, carry):
        @pl.when(me > 0)
        def _():
            halo(0, chunk, me - 1).wait_send()

        @pl.when(me < bands - 1)
        def _():
            halo(1, chunk, me + 1).wait_send()

        return carry

    lax.fori_loop(0, CHUNKS, end, 0)


def peers(axis, send):
    size = lax.axis_size(axis)
    me = lax.axis_index(axis)
    for d in range(1, size):
        send(lax.rem(me + d, size), d)


def exchange(axis, mine_ref, slots_ref, send_sem, recv_sem):
    me = lax.axis_index(axis)

    def copy(other, slot, d):
        return pltpu.make_async_remote_copy(
            src_ref=mine_ref,
            dst_ref=slots_ref.at[slot],
            send_sem=send_sem.at[d],
            recv_sem=recv_sem.at[slot],
            device_id={axis: other},
            device_id_type=pl.DeviceIdType.MESH,
        )

    peers(axis, lambda other, d: copy(other, me, d).start())
    slots_ref[me] = mine_ref[...]
    peers(axis, lambda other, d: copy(other, other, d).wait_recv())
    peers(axis, lambda other, d: copy(other, me, d).wait_send())


def greet(axes):
    barrier = pltpu.get_barrier_semaphore()
    for axis in axes:
        peers(
            axis,
            lambda other, d: pl.semaphore_signal(
                barrier, inc=1, device_id={axis: other}, device_id_type=pl.DeviceIdType.MESH
            ),
        )
    pl.semaphore_wait(barrier, sum(lax.axis_size(axis) - 1 for axis in axes))


def finish_kernel(
    tq_ref, land_ref, b_hi_ref, b_lo_ref, head_ref, out_ref,
    first_ref, last_ref, below_ref, above_ref, part_ref, mine_ref, lat_slots, sum_ref, grp_slots,
    edge_send, edge_recv, lat_send, lat_recv, grp_send, grp_recv,
):
    members, _, own, lon = tq_ref.shape
    me, size = lax.axis_index("lat"), lax.axis_size("lat")
    for m in range(members):
        for k in range(2):
            at = 2 * m + k
            first_ref[at : at + 1, :] = tq_ref[m, k, 0:1, :]
            last_ref[at : at + 1, :] = tq_ref[m, k, own - 1 : own, :]
    greet(("lat", "grp"))

    def edge(way, other):
        return pltpu.make_async_remote_copy(
            src_ref=(first_ref, last_ref)[way],
            dst_ref=(below_ref, above_ref)[way],
            send_sem=edge_send.at[way],
            recv_sem=edge_recv.at[way],
            device_id={"lat": other},
            device_id_type=pl.DeviceIdType.MESH,
        )

    @pl.when(me > 0)
    def _():
        edge(0, me - 1).start()

    @pl.when(me < size - 1)
    def _():
        edge(1, me + 1).start()

    @pl.when(me > 0)
    def _():
        edge(1, me - 1).wait_recv()
        edge(0, me - 1).wait_send()

    @pl.when(me < size - 1)
    def _():
        edge(0, me + 1).wait_recv()
        edge(1, me + 1).wait_send()

    @pl.when(me == 0)
    def _():
        above_ref[...] = jnp.zeros_like(above_ref)

    @pl.when(me == size - 1)
    def _():
        below_ref[...] = jnp.zeros_like(below_ref)

    land = land_ref[...]
    pad = b_hi_ref.shape[1] - 9 * (own + SUB)
    place = lax.broadcasted_iota(jnp.int32, (SUB, lon), 0)

    def pair(i, carry):
        highs, lows = [], []
        for g in range(2):
            values = []
            for k in range(2):
                at = 4 * i + 2 * g + k
                ext = jnp.where(
                    place == 0,
                    below_ref[pl.ds(at, 1), :],
                    jnp.where(place == SUB - 1, above_ref[pl.ds(at, 1), :], 0.0),
                )
                values.append(jnp.concatenate([tq_ref[2 * i + g, k], ext], axis=0))
            t, q = values
            rows = []
            for value in (t * land, q, t * (1.0 - land)):
                rows += [pltpu.roll(value, 1, 1), value, pltpu.roll(value, lon - 1, 1)]
            if pad:
                rows.append(jnp.zeros((pad, lon), F32))
            hi, lo = split_hi_lo(jnp.concatenate(rows, axis=0))
            highs.append(hi)
            lows.append(lo)
        hidden = dot3(
            b_hi_ref[...], b_lo_ref[...], jnp.concatenate(highs, axis=1), jnp.concatenate(lows, axis=1)
        )
        hidden = jnp.maximum(hidden, 0.0)
        for g in range(2):
            terms = hidden[:, g * lon : (g + 1) * lon] * head_ref[...]
            part_ref[pl.ds(2 * i + g, 1), :] = jnp.sum(terms, axis=0, keepdims=True)
        return carry

    lax.fori_loop(0, members // 2, pair, 0)
    total = jnp.sum(part_ref[...], axis=1, keepdims=True)
    row = lax.broadcasted_iota(jnp.int32, (members, lon), 0)
    col = lax.broadcasted_iota(jnp.int32, (members, lon), 1)
    flat = jnp.sum(jnp.where(row == col, total, 0.0), axis=0, keepdims=True)
    mine_ref[...] = jnp.broadcast_to(flat, mine_ref.shape)
    exchange("lat", mine_ref, lat_slots, lat_send, lat_recv)
    score = lat_slots[0]
    for k in range(1, size):
        score = score + lat_slots[k]
    sum_ref[...] = score
    exchange("grp", sum_ref, grp_slots, grp_send, grp_recv)
    out_ref[...] = grp_slots[...]


def params():
    return pltpu.CompilerParams(vmem_limit_bytes=40 * 2**20)


def full_spec(array):
    zeros = (0,) * array.ndim
    return pl.BlockSpec(array.shape, lambda *_: zeros)


def steps_scratch(members, levels, rows, lon):
    width = members * (rows // SUB) * lon
    return [
        pltpu.VMEM((members, levels, rows, lon), F32),
        pltpu.VMEM((levels * SUB, width), BF16),
        pltpu.VMEM((levels * SUB, width), BF16),
    ]


def run_donor(donor, below, above, consts):
    _, levels, own, lon = donor.shape
    ins = (donor, below, above) + consts
    return pl.pallas_call(
        donor_kernel,
        out_shape=jax.ShapeDtypeStruct(donor.shape, F32),
        in_specs=[full_spec(a) for a in ins],
        out_specs=full_spec(donor),
        grid=(1,),
        scratch_shapes=steps_scratch(1, levels, own + EXT, lon),
        compiler_params=params(),
        name="donor_steps",
    )(*ins)


def run_main(fields, consts):
    members, levels, own, lon = fields.shape
    group = 2
    ins = (fields, fields[:, :, :STEPS], fields[:, :, own - STEPS :]) + consts
    halo = pltpu.VMEM((members, levels, STEPS, lon), F32)
    flops = 6 * members * levels * levels * SUB * (own + EXT) * lon * STEPS
    return pl.pallas_call(
        main_kernel,
        out_shape=(
            jax.ShapeDtypeStruct(fields.shape, F32),
            jax.ShapeDtypeStruct((members, 2, own, lon), F32),
        ),
        in_specs=[pl.BlockSpec(memory_space=pltpu.VMEM)] * len(ins),
        out_specs=(pl.BlockSpec(memory_space=pltpu.VMEM),) * 2,
        scratch_shapes=[halo, halo]
        + steps_scratch(group, levels, own + EXT, lon)
        + [pltpu.SemaphoreType.DMA((2, CHUNKS)), pltpu.SemaphoreType.DMA((2, CHUNKS))],
        compiler_params=pltpu.CompilerParams(
            collective_id=1, has_side_effects=True, vmem_limit_bytes=56 * 2**20
        ),
        cost_estimate=pl.CostEstimate(
            flops=10 * flops, bytes_accessed=3 * members * levels * own * lon * 4, transcendentals=0
        ),
        name="main_steps",
    )(*ins)


def run_finish(tq, land, b_hi, b_lo, head):
    members, _, own, lon = tq.shape
    lat, grp = lax.axis_size("lat"), lax.axis_size("grp")
    edge = pltpu.VMEM((2 * members, lon), F32)
    tile = pltpu.VMEM((SUB, lon), F32)
    return pl.pallas_call(
        finish_kernel,
        out_shape=jax.ShapeDtypeStruct((grp, SUB, lon), F32),
        in_specs=[pl.BlockSpec(memory_space=pltpu.VMEM)] * 5,
        out_specs=pl.BlockSpec(memory_space=pltpu.VMEM),
        scratch_shapes=[
            edge, edge, edge, edge,
            pltpu.VMEM((members, lon), F32),
            tile,
            pltpu.VMEM((lat, SUB, lon), F32),
            tile,
            pltpu.VMEM((grp, SUB, lon), F32),
            pltpu.SemaphoreType.DMA((2,)),
            pltpu.SemaphoreType.DMA((2,)),
            pltpu.SemaphoreType.DMA((lat,)),
            pltpu.SemaphoreType.DMA((lat,)),
            pltpu.SemaphoreType.DMA((grp,)),
            pltpu.SemaphoreType.DMA((grp,)),
        ],
        compiler_params=pltpu.CompilerParams(
            collective_id=0, has_side_effects=True, vmem_limit_bytes=40 * 2**20
        ),
        name="finish",
    )(tq, land, b_hi, b_lo, head)


def halos(value, dim, width, axis="lat"):
    size, length = lax.axis_size(axis), value.shape[dim]
    up = [(i, i + 1) for i in range(size - 1)]
    down = [(j, i) for i, j in up]
    above = lax.ppermute(lax.slice_in_dim(value, length - width, length, axis=dim), axis, up)
    below = lax.ppermute(lax.slice_in_dim(value, 0, width, axis=dim), axis, down)
    return below, above


def conv_matrix(conv_weight, own):
    rows = own + SUB
    channels = conv_weight.shape[0]
    taps = conv_weight.reshape(channels, 1, 3, 3, 3, 1)
    i = jnp.arange(own)[:, None, None]
    a = jnp.arange(3)[None, :, None]
    r = jnp.arange(rows)[None, None, :]
    hit = ((i + a - 1) % rows == r).astype(F32)
    parts = [taps[:, :, :, k] * hit[None, :, None, None, k, :] for k in range(3)]
    matrix = (parts[0] + parts[1] + parts[2]).reshape(channels * own, 9 * rows)
    pad = -matrix.shape[1] % 16
    return jnp.pad(matrix, ((0, 0), (0, pad)))


def local(fields, diffusion, mixing, heating, land_mask, conv_weight, head_weight, counts, source):
    members, levels, own, lon = fields.shape
    total_members = counts.shape[0]
    me = lax.axis_index("grp")
    offset = me * members
    local_counts = lax.dynamic_slice_in_dim(counts, offset, members)
    local_source = lax.dynamic_slice_in_dim(source, offset, members)
    killed = (local_source != offset + jnp.arange(members, dtype=jnp.int32)).astype(jnp.int32)
    donor_group = jnp.max(jnp.where(killed > 0, local_source // members, 0))

    land = land_mask.astype(F32)
    hot = lax.dynamic_index_in_dim(fields, jnp.argmax(local_counts), 0, keepdims=False)
    stack = jnp.concatenate([hot, heating, diffusion[None], land[None]], axis=0)
    stack_all = jnp.concatenate([stack, *halos(stack, 1, STEPS)], axis=1)
    hot_all, heat_all = stack_all[:levels], stack_all[levels : 2 * levels]
    diff_all, land_all = stack_all[2 * levels], stack_all[2 * levels + 1]
    gathered = lax.all_gather(hot_all, "grp", axis=0)
    donor_all = lax.dynamic_index_in_dim(gathered, donor_group, 0, keepdims=True)
    eye = jnp.eye(SUB, dtype=F32)
    wide = (mixing[:, None, :, None] * eye[None, :, None, :]).reshape(levels * SUB, levels * SUB)
    consts = (diff_all, heat_all, *split_constant(wide))

    donor = run_donor(
        donor_all[:, :, :own],
        donor_all[:, :, own : own + STEPS],
        donor_all[:, :, own + STEPS :],
        consts,
    )
    final, tq = run_main(fields, consts)
    new_fields = jnp.where(killed[:, None, None, None] > 0, donor, final)
    b_hi, b_lo = split_constant(conv_matrix(conv_weight, own))
    table = run_finish(tq, land_all, b_hi, b_lo, head_weight.reshape(-1, lon))
    all_scores = table[:, 0, :members].reshape(total_members)
    scores = lax.dynamic_slice_in_dim(all_scores, offset, members)
    weights = jnp.exp(all_scores)
    weights = weights / jnp.mean(weights)
    selector = (local_source[:, None] == jnp.arange(total_members, dtype=jnp.int32)[None, :]).astype(F32)
    chosen_weight = jnp.sum(selector * weights[None, :], 1)
    chosen_count = jnp.sum(selector * counts.astype(F32)[None, :], 1)
    return new_fields, scores, chosen_weight / chosen_count


def solution(mesh):
    return jax.shard_map(
        local,
        mesh=mesh,
        in_specs=(
            P("grp", None, "lat", None),
            P("lat", None),
            P(),
            P(None, "lat", None),
            P("lat", None),
            P(),
            P(None, "lat", None),
            P(),
            P(),
        ),
        out_specs=(P("grp", None, "lat", None), P("grp"), P("grp")),
        check_vma=False,
    )
```

```python
import functools
import jax
import jax.numpy as jnp
from jax import lax
from jax.experimental import pallas as pl
from jax.experimental.pallas import tpu as pltpu
from jax.sharding import PartitionSpec as P

LEV = 10
STEPS = 4
SUB = 8
CHUNKS = 8
EXT = 2 * STEPS
F32 = jnp.float32
BF16 = jnp.bfloat16


def split_hi_lo(value):
    hi = value.astype(BF16)
    lo = (value - hi.astype(F32)).astype(BF16)
    return hi, lo


def split_constant(value):
    hi = lax.reduce_precision(value, 8, 7)
    return hi.astype(BF16), (value - hi).astype(BF16)


def dot3(a_hi, a_lo, b_hi, b_lo):
    dot = functools.partial(jnp.dot, preferred_element_type=F32)
    return dot(a_hi, b_hi) + (dot(a_hi, b_lo) + dot(a_lo, b_hi))


def steps_body(fields_ref, below_ref, above_ref, diff_ref, heat_ref, w_hi_ref, w_lo_ref, x_ref, y_hi_ref, y_lo_ref):
    members, levels, rows, lon = x_ref.shape
    own = rows - EXT
    tiles = rows // SUB
    width = members * tiles * lon
    cols = min(2 * lon, width)
    x_ref[:, :, :own, :] = fields_ref[...]
    x_ref[:, :, own : own + STEPS, :] = below_ref[...]
    x_ref[:, :, own + STEPS :, :] = above_ref[...]
    place = lax.broadcasted_iota(jnp.int32, (1, SUB, lon), 1)
    depth = jnp.where(place < STEPS, place, SUB - 1 - place)

    def one_step(step, carry):
        for g in range(members):
            for f in range(0, levels, 2):
                x = x_ref[g, f : f + 2]
                near = (
                    pltpu.roll(x, 1, 1)
                    + pltpu.roll(x, rows - 1, 1)
                    + pltpu.roll(x, 1, 2)
                    + pltpu.roll(x, lon - 1, 2)
                    - 4.0 * x
                )
                y = x + diff_ref[...][None] * near
                for t in range(tiles):
                    part = y[:, SUB * t : SUB * (t + 1), :].reshape(2 * SUB, lon)
                    hi, lo = split_hi_lo(part)
                    at = (g * tiles + t) * lon
                    y_hi_ref[SUB * f : SUB * (f + 2), at : at + lon] = hi
                    y_lo_ref[SUB * f : SUB * (f + 2), at : at + lon] = lo
        for start in range(0, width, cols):
            end = min(start + cols, width)
            z = dot3(w_hi_ref[...], w_lo_ref[...], y_hi_ref[:, start:end], y_lo_ref[:, start:end])
            for at in range(start, end, lon):
                g, t = divmod(at // lon, tiles)
                mixed = z[:, at - start : at - start + lon].reshape(levels, SUB, lon)
                new = mixed + heat_ref[:, SUB * t : SUB * (t + 1), :] - 0.05 * mixed * mixed * mixed
                if t == tiles - 1:
                    new = jnp.where(depth < STEPS - 1 - step, new, 0.0)
                x_ref[g, :, SUB * t : SUB * (t + 1), :] = new
        return carry

    lax.fori_loop(0, STEPS, one_step, 0)


def donor_kernel(fields_ref, below_ref, above_ref, diff_ref, heat_ref, w_hi_ref, w_lo_ref, out_ref, x_ref, y_hi_ref, y_lo_ref):
    steps_body(fields_ref, below_ref, above_ref, diff_ref, heat_ref, w_hi_ref, w_lo_ref, x_ref, y_hi_ref, y_lo_ref)
    out_ref[...] = x_ref[:, :, : out_ref.shape[2], :]


def main_kernel(
    fields_ref, low_ref, high_ref, diff_ref, heat_ref, w_hi_ref, w_lo_ref, out_ref, tq_ref,
    below_ref, above_ref, x_ref, y_hi_ref, y_lo_ref, send_sem, recv_sem,
):
    members, levels, own, lon = out_ref.shape
    group = x_ref.shape[0]
    size = members // CHUNKS
    me, bands = lax.axis_index("lat"), lax.axis_size("lat")

    def halo(way, chunk, other):
        part = pl.ds(chunk * size, size)
        return pltpu.make_async_remote_copy(
            src_ref=(low_ref, high_ref)[way].at[part],
            dst_ref=(below_ref, above_ref)[way].at[part],
            send_sem=send_sem.at[way, chunk],
            recv_sem=recv_sem.at[way, chunk],
            device_id={"lat": other},
            device_id_type=pl.DeviceIdType.MESH,
        )

    greet(("lat",))

    def begin(chunk, carry):
        @pl.when(me > 0)
        def _():
            halo(0, chunk, me - 1).start()

        @pl.when(me < bands - 1)
        def _():
            halo(1, chunk, me + 1).start()

        return carry

    lax.fori_loop(0, CHUNKS, begin, 0)

    @pl.when(me == 0)
    def _():
        above_ref[...] = jnp.zeros_like(above_ref)

    @pl.when(me == bands - 1)
    def _():
        below_ref[...] = jnp.zeros_like(below_ref)

    def work(chunk, carry):
        @pl.when(me > 0)
        def _():
            halo(1, chunk, me - 1).wait_recv()

        @pl.when(me < bands - 1)
        def _():
            halo(0, chunk, me + 1).wait_recv()

        def few(i, inner):
            part = pl.ds(chunk * size + i * group, group)
            steps_body(
                fields_ref.at[part], below_ref.at[part], above_ref.at[part],
                diff_ref, heat_ref, w_hi_ref, w_lo_ref, x_ref, y_hi_ref, y_lo_ref,
            )
            out_ref[part] = x_ref[:, :, :own, :]
            tq_ref[part, 0] = x_ref[:, 0, :own, :]
            tq_ref[part, 1] = x_ref[:, LEV, :own, :]
            return inner

        lax.fori_loop(0, size // group, few, 0)
        return carry

    lax.fori_loop(0, CHUNKS, work, 0)

    def end(chunk, carry):
        @pl.when(me > 0)
        def _():
            halo(0, chunk, me - 1).wait_send()

        @pl.when(me < bands - 1)
        def _():
            halo(1, chunk, me + 1).wait_send()

        return carry

    lax.fori_loop(0, CHUNKS, end, 0)


def peers(axis, send):
    size = lax.axis_size(axis)
    me = lax.axis_index(axis)
    for d in range(1, size):
        send(lax.rem(me + d, size), d)


def exchange(axis, mine_ref, slots_ref, send_sem, recv_sem):
    me = lax.axis_index(axis)

    def copy(other, slot, d):
        return pltpu.make_async_remote_copy(
            src_ref=mine_ref,
            dst_ref=slots_ref.at[slot],
            send_sem=send_sem.at[d],
            recv_sem=recv_sem.at[slot],
            device_id={axis: other},
            device_id_type=pl.DeviceIdType.MESH,
        )

    peers(axis, lambda other, d: copy(other, me, d).start())
    slots_ref[me] = mine_ref[...]
    peers(axis, lambda other, d: copy(other, other, d).wait_recv())
    peers(axis, lambda other, d: copy(other, me, d).wait_send())


def greet(axes):
    barrier = pltpu.get_barrier_semaphore()
    for axis in axes:
        peers(
            axis,
            lambda other, d: pl.semaphore_signal(
                barrier, inc=1, device_id={axis: other}, device_id_type=pl.DeviceIdType.MESH
            ),
        )
    pl.semaphore_wait(barrier, sum(lax.axis_size(axis) - 1 for axis in axes))


def finish_kernel(
    tq_ref, land_ref, b_hi_ref, b_lo_ref, head_ref, out_ref,
    first_ref, last_ref, below_ref, above_ref, part_ref, mine_ref, lat_slots, sum_ref, grp_slots,
    edge_send, edge_recv, lat_send, lat_recv, grp_send, grp_recv,
):
    members, _, own, lon = tq_ref.shape
    me, size = lax.axis_index("lat"), lax.axis_size("lat")
    for m in range(members):
        for k in range(2):
            at = 2 * m + k
            first_ref[at : at + 1, :] = tq_ref[m, k, 0:1, :]
            last_ref[at : at + 1, :] = tq_ref[m, k, own - 1 : own, :]
    greet(("lat", "grp"))

    def edge(way, other):
        return pltpu.make_async_remote_copy(
            src_ref=(first_ref, last_ref)[way],
            dst_ref=(below_ref, above_ref)[way],
            send_sem=edge_send.at[way],
            recv_sem=edge_recv.at[way],
            device_id={"lat": other},
            device_id_type=pl.DeviceIdType.MESH,
        )

    @pl.when(me > 0)
    def _():
        edge(0, me - 1).start()

    @pl.when(me < size - 1)
    def _():
        edge(1, me + 1).start()

    @pl.when(me > 0)
    def _():
        edge(1, me - 1).wait_recv()
        edge(0, me - 1).wait_send()

    @pl.when(me < size - 1)
    def _():
        edge(0, me + 1).wait_recv()
        edge(1, me + 1).wait_send()

    @pl.when(me == 0)
    def _():
        above_ref[...] = jnp.zeros_like(above_ref)

    @pl.when(me == size - 1)
    def _():
        below_ref[...] = jnp.zeros_like(below_ref)

    land = land_ref[...]
    pad = b_hi_ref.shape[1] - 9 * (own + SUB)
    place = lax.broadcasted_iota(jnp.int32, (SUB, lon), 0)

    def pair(i, carry):
        highs, lows = [], []
        for g in range(2):
            values = []
            for k in range(2):
                at = 4 * i + 2 * g + k
                ext = jnp.where(
                    place == 0,
                    below_ref[pl.ds(at, 1), :],
                    jnp.where(place == SUB - 1, above_ref[pl.ds(at, 1), :], 0.0),
                )
                values.append(jnp.concatenate([tq_ref[2 * i + g, k], ext], axis=0))
            t, q = values
            rows = []
            for value in (t * land, q, t * (1.0 - land)):
                rows += [pltpu.roll(value, 1, 1), value, pltpu.roll(value, lon - 1, 1)]
            if pad:
                rows.append(jnp.zeros((pad, lon), F32))
            hi, lo = split_hi_lo(jnp.concatenate(rows, axis=0))
            highs.append(hi)
            lows.append(lo)
        hidden = dot3(
            b_hi_ref[...], b_lo_ref[...], jnp.concatenate(highs, axis=1), jnp.concatenate(lows, axis=1)
        )
        hidden = jnp.maximum(hidden, 0.0)
        for g in range(2):
            terms = hidden[:, g * lon : (g + 1) * lon] * head_ref[...]
            part_ref[pl.ds(2 * i + g, 1), :] = jnp.sum(terms, axis=0, keepdims=True)
        return carry

    lax.fori_loop(0, members // 2, pair, 0)
    total = jnp.sum(part_ref[...], axis=1, keepdims=True)
    row = lax.broadcasted_iota(jnp.int32, (members, lon), 0)
    col = lax.broadcasted_iota(jnp.int32, (members, lon), 1)
    flat = jnp.sum(jnp.where(row == col, total, 0.0), axis=0, keepdims=True)
    mine_ref[...] = jnp.broadcast_to(flat, mine_ref.shape)
    exchange("lat", mine_ref, lat_slots, lat_send, lat_recv)
    score = lat_slots[0]
    for k in range(1, size):
        score = score + lat_slots[k]
    sum_ref[...] = score
    exchange("grp", sum_ref, grp_slots, grp_send, grp_recv)
    out_ref[...] = grp_slots[...]


def params():
    return pltpu.CompilerParams(vmem_limit_bytes=40 * 2**20)


def full_spec(array):
    zeros = (0,) * array.ndim
    return pl.BlockSpec(array.shape, lambda *_: zeros)


def steps_scratch(members, levels, rows, lon):
    width = members * (rows // SUB) * lon
    return [
        pltpu.VMEM((members, levels, rows, lon), F32),
        pltpu.VMEM((levels * SUB, width), BF16),
        pltpu.VMEM((levels * SUB, width), BF16),
    ]


def run_donor(donor, below, above, consts):
    _, levels, own, lon = donor.shape
    ins = (donor, below, above) + consts
    return pl.pallas_call(
        donor_kernel,
        out_shape=jax.ShapeDtypeStruct(donor.shape, F32),
        in_specs=[full_spec(a) for a in ins],
        out_specs=full_spec(donor),
        grid=(1,),
        scratch_shapes=steps_scratch(1, levels, own + EXT, lon),
        compiler_params=params(),
        name="donor_steps",
    )(*ins)


def run_main(fields, consts):
    members, levels, own, lon = fields.shape
    group = 2
    ins = (fields, fields[:, :, :STEPS], fields[:, :, own - STEPS :]) + consts
    halo = pltpu.VMEM((members, levels, STEPS, lon), F32)
    flops = 6 * members * levels * levels * SUB * (own + EXT) * lon * STEPS
    return pl.pallas_call(
        main_kernel,
        out_shape=(
            jax.ShapeDtypeStruct(fields.shape, F32),
            jax.ShapeDtypeStruct((members, 2, own, lon), F32),
        ),
        in_specs=[pl.BlockSpec(memory_space=pltpu.VMEM)] * len(ins),
        out_specs=(pl.BlockSpec(memory_space=pltpu.VMEM),) * 2,
        scratch_shapes=[halo, halo]
        + steps_scratch(group, levels, own + EXT, lon)
        + [pltpu.SemaphoreType.DMA((2, CHUNKS)), pltpu.SemaphoreType.DMA((2, CHUNKS))],
        compiler_params=pltpu.CompilerParams(
            collective_id=1, has_side_effects=True, vmem_limit_bytes=56 * 2**20
        ),
        cost_estimate=pl.CostEstimate(
            flops=10 * flops, bytes_accessed=3 * members * levels * own * lon * 4, transcendentals=0
        ),
        name="main_steps",
    )(*ins)


def run_finish(tq, land, b_hi, b_lo, head):
    members, _, own, lon = tq.shape
    lat, grp = lax.axis_size("lat"), lax.axis_size("grp")
    edge = pltpu.VMEM((2 * members, lon), F32)
    tile = pltpu.VMEM((SUB, lon), F32)
    return pl.pallas_call(
        finish_kernel,
        out_shape=jax.ShapeDtypeStruct((grp, SUB, lon), F32),
        in_specs=[pl.BlockSpec(memory_space=pltpu.VMEM)] * 5,
        out_specs=pl.BlockSpec(memory_space=pltpu.VMEM),
        scratch_shapes=[
            edge, edge, edge, edge,
            pltpu.VMEM((members, lon), F32),
            tile,
            pltpu.VMEM((lat, SUB, lon), F32),
            tile,
            pltpu.VMEM((grp, SUB, lon), F32),
            pltpu.SemaphoreType.DMA((2,)),
            pltpu.SemaphoreType.DMA((2,)),
            pltpu.SemaphoreType.DMA((lat,)),
            pltpu.SemaphoreType.DMA((lat,)),
            pltpu.SemaphoreType.DMA((grp,)),
            pltpu.SemaphoreType.DMA((grp,)),
        ],
        compiler_params=pltpu.CompilerParams(
            collective_id=0, has_side_effects=True, vmem_limit_bytes=40 * 2**20
        ),
        name="finish",
    )(tq, land, b_hi, b_lo, head)


def halos(value, dim, width, axis="lat"):
    size, length = lax.axis_size(axis), value.shape[dim]
    up = [(i, i + 1) for i in range(size - 1)]
    down = [(j, i) for i, j in up]
    above = lax.ppermute(lax.slice_in_dim(value, length - width, length, axis=dim), axis, up)
    below = lax.ppermute(lax.slice_in_dim(value, 0, width, axis=dim), axis, down)
    return below, above


def spread(value, width, run):
    col = lax.broadcasted_iota(jnp.int32, (value.shape[1], width), 1)
    row = lax.broadcasted_iota(jnp.int32, (value.shape[1], width), 0)
    return jnp.dot(value, (col // run == row).astype(F32), precision=lax.Precision.HIGHEST)


def conv_matrix(conv_weight, own):
    rows = own + SUB
    channels = conv_weight.shape[0]
    width = 9 * rows + (-9 * rows) % 16
    taps = conv_weight.reshape(channels, 3, 3, 3).transpose(2, 0, 1, 3).reshape(3 * channels, 9)
    taps = spread(taps, width, rows).reshape(3, channels, 1, width)
    i = lax.broadcasted_iota(jnp.int32, (1, own, width), 1)
    r = lax.broadcasted_iota(jnp.int32, (1, own, width), 2) % rows
    parts = [jnp.where((i + a - 1 + rows) % rows == r, taps[a], 0.0) for a in range(3)]
    return (parts[0] + parts[1] + parts[2]).reshape(channels * own, width)


def mixing_matrix(mixing):
    levels = mixing.shape[0]
    i = lax.broadcasted_iota(jnp.int32, (1, SUB, levels * SUB), 1)
    r = lax.broadcasted_iota(jnp.int32, (1, SUB, levels * SUB), 2) % SUB
    wide = jnp.where(i == r, spread(mixing, levels * SUB, SUB)[:, None, :], 0.0)
    return wide.reshape(levels * SUB, levels * SUB)


def local(fields, diffusion, mixing, heating, land_mask, conv_weight, head_weight, counts, source):
    members, levels, own, lon = fields.shape
    total_members = counts.shape[0]
    me = lax.axis_index("grp")
    offset = me * members
    local_counts = lax.dynamic_slice_in_dim(counts, offset, members)
    local_source = lax.dynamic_slice_in_dim(source, offset, members)
    killed = (local_source != offset + jnp.arange(members, dtype=jnp.int32)).astype(jnp.int32)
    donor_group = jnp.max(jnp.where(killed > 0, local_source // members, 0))

    land = land_mask.astype(F32)
    hot = lax.dynamic_index_in_dim(fields, jnp.argmax(local_counts), 0, keepdims=False)
    stack = jnp.concatenate([hot, heating, diffusion[None], land[None]], axis=0)
    stack_all = jnp.concatenate([stack, *halos(stack, 1, STEPS)], axis=1)
    hot_all, heat_all = stack_all[:levels], stack_all[levels : 2 * levels]
    diff_all, land_all = stack_all[2 * levels], stack_all[2 * levels + 1]
    gathered = lax.all_gather(hot_all, "grp", axis=0)
    donor_all = lax.dynamic_index_in_dim(gathered, donor_group, 0, keepdims=True)
    consts = (diff_all, heat_all, *split_constant(mixing_matrix(mixing)))

    donor = run_donor(
        donor_all[:, :, :own],
        donor_all[:, :, own : own + STEPS],
        donor_all[:, :, own + STEPS :],
        consts,
    )
    final, tq = run_main(fields, consts)
    new_fields = jnp.where(killed[:, None, None, None] > 0, donor, final)
    b_hi, b_lo = split_constant(conv_matrix(conv_weight, own))
    table = run_finish(tq, land_all, b_hi, b_lo, head_weight.reshape(-1, lon))
    all_scores = table[:, 0, :members].reshape(total_members)
    scores = lax.dynamic_slice_in_dim(all_scores, offset, members)
    weights = jnp.exp(all_scores)
    weights = weights / jnp.mean(weights)
    selector = (local_source[:, None] == jnp.arange(total_members, dtype=jnp.int32)[None, :]).astype(F32)
    chosen_weight = jnp.sum(selector * weights[None, :], 1)
    chosen_count = jnp.sum(selector * counts.astype(F32)[None, :], 1)
    return new_fields, scores, chosen_weight / chosen_count


def solution(mesh):
    return jax.shard_map(
        local,
        mesh=mesh,
        in_specs=(
            P("grp", None, "lat", None),
            P("lat", None),
            P(),
            P(None, "lat", None),
            P("lat", None),
            P(),
            P(None, "lat", None),
            P(),
            P(),
        ),
        out_specs=(P("grp", None, "lat", None), P("grp"), P("grp")),
        check_vma=False,
    )
```
